32 devices in a mesh: image: 8 (over y, x, core), space: 4 (over z).
Axes of the slice: x: 2, y: 2, z: 4, core: 2. Of those that a mesh axis runs over, the one named last changes fastest.
Arguments:
- coords: float32 [16, 3, 32768], P('image', None, 'space'), may hold values from -16 to 16
- ref_coords: float32 [3, 32768], P(None, 'space'), may hold values from -4 to 4
- restraint: float32 [32768], P('space'), may hold values from 0.5 to 5
- atom_types: int32 [32768], P('space'), may hold values from 0 to 63
- well_table: float32 [64], replicated, may hold values from 0.3 to 1.5
- radius_table: float32 [64], replicated, may hold values from 0.4 to 1
- tile_lists: int32 [16, 4, 256], P('image', None, 'space'), may hold values from 0 to 79
- halo_index: int32 [16, 2, 4096], P('image', None, 'space'), may hold values from 0 to 8191
Outputs:
- neb_force: float32 [16, 3, 32768], P('image', None, 'space')
- energies: float32 [16], P('image')
The draws below stay inside these ranges and needn't reach their ends.
All inputs are finite; a program needn't handle non-finite values.
Results may differ from the reference program's by a relative error of at most 0.0001.
Values sent between devices are 32-bit elements; how exact they have to be, the bound alone decides.
A program may use at most 64 MiB of HBM per device.

```python
import math
import jax
import jax.numpy as jnp
from jax import lax

ATOMS_DEV = 8192
HALO = 1024
PARTNERS = 4
NTYPES = 64
TILE = 128
NT_EXT = 80
IMAGES = 16
ATOMS = 32768
TILES = 256
HALOS = 4096
N_SPACE = 4


def common_layout(key):
    position = jnp.arange(ATOMS, dtype=jnp.float32) / ATOMS
    base = jnp.clip(jax.random.normal(jax.random.fold_in(key, 11), (3, ATOMS), jnp.float32), -4.0, 4.0)
    base = base * 0.6 * (1.6 - 0.8 * position)
    path = jnp.clip(jax.random.normal(jax.random.fold_in(key, 12), (3, ATOMS), jnp.float32), -4.0, 4.0)
    spread = jnp.exp(jax.random.uniform(jax.random.fold_in(key, 13), (ATOMS,), jnp.float32, math.log(0.2), math.log(2.0)))
    spread = spread * (1.0 + 2.0 * position) / 2.0
    return (base, path, spread)


def draw_coords(key, part):
    base, path, spread = common_layout(key)
    scales = jnp.exp(jax.random.uniform(jax.random.fold_in(key, 14), (IMAGES, 1, 1), jnp.float32, math.log(0.3), math.log(3.0)))
    noise = jnp.clip(jax.random.normal(jax.random.fold_in(key, 15), (IMAGES, 3, ATOMS), jnp.float32), -4.0, 4.0)
    return base[None] + 0.3 * scales * path[None] * spread + 0.1 * noise * spread


def draw_ref_coords(key, part):
    base, path, spread = common_layout(key)
    return base


def draw_tile_lists(key, part):
    values = jax.random.randint(key, (IMAGES, PARTNERS, TILES), 0, NT_EXT, jnp.int32)
    return values.at[0, 0, 0].set(NT_EXT - 1).at[0, 1, 0].set(0)


def draw_halo_index(key, part):
    values = jax.random.randint(key, (IMAGES, 2, HALOS), 0, ATOMS_DEV, jnp.int32)
    return values.at[0, 0, 0].set(ATOMS_DEV - 1).at[0, 0, 1].set(0)


def set_ends(drawn, own_key, low, largest):
    shape = drawn.shape
    spot = [jax.random.randint(jax.random.fold_in(own_key, axis), (), 0, shape[axis]) for axis in range(len(shape))]
    drawn = drawn.at[tuple(spot)].set(low)
    longest = shape.index(max(shape))
    spot[longest] = (spot[longest] + 1) % shape[longest]
    return drawn.at[tuple(spot)].set(largest)


def block_levels(rng, dims, shards, smallest, top_value):
    gain, own = 1.0, jax.random.fold_in(rng, 6)
    for dim, parts in shards:
        steps = jnp.exp(jax.random.uniform(jax.random.fold_in(own, dim), (parts,), jnp.float32, smallest / len(shards), top_value / len(shards)))
        gain = gain * jnp.repeat(steps, dims[dim] // parts).reshape([-1 if axis == dim else 1 for axis in range(len(dims))])
    return gain


def setup_inputs(seed: int = 0) -> dict:
    key_list = jax.random.split(jax.random.key(seed), 9)
    coords = draw_coords(jax.random.fold_in(key_list[8], 71), 0)
    ref_coords = draw_ref_coords(jax.random.fold_in(key_list[8], 71), 0)
    restraint = jnp.clip(jnp.exp(math.log(5.0) - 2.3025851 * jax.random.uniform(key_list[2], (ATOMS,), jnp.float32) ** block_levels(key_list[2], (ATOMS,), ((0, 4),), -0.2, 0.2)), 0.5, 5.0)
    atom_types = set_ends(jax.random.randint(key_list[3], (ATOMS,), 0, NTYPES), jax.random.fold_in(key_list[3], 1), 0, NTYPES - 1).astype(jnp.int32)
    well_table = jnp.clip(jnp.exp(jax.random.uniform(key_list[4], (NTYPES,), jnp.float32, math.log(0.3), math.log(1.5))), 0.3, 1.5)
    radius_table = jnp.clip(jnp.exp(jax.random.uniform(key_list[5], (NTYPES,), jnp.float32, math.log(0.4), math.log(1.0))), 0.4, 1.0)
    tile_lists = draw_tile_lists(jax.random.fold_in(key_list[8], 71), 0)
    halo_index = draw_halo_index(jax.random.fold_in(key_list[8], 71), 0)
    return {"coords": coords, "ref_coords": ref_coords, "restraint": restraint, "atom_types": atom_types, "well_table": well_table, "radius_table": radius_table, "tile_lists": tile_lists, "halo_index": halo_index}


soft_core = 1.0
spring_k = 2.0
small_eps = 1e-06

def pair_terms(own, partner):
    delta = own[:3, ..., :, None] - partner[:3, ..., None, :]
    dist_sq = lax.optimization_barrier(jnp.sum(delta * delta, axis=0))
    reach = own[4, ..., :, None] + partner[4, ..., None, :]
    reach_sq = reach * reach
    ratio = reach_sq / (dist_sq + soft_core * reach_sq)
    cubed = ratio * ratio * ratio
    strength = own[3, ..., :, None] * partner[3, ..., None, :]
    energy = lax.optimization_barrier(jnp.sum(4.0 * strength * (cubed * cubed - cubed), axis=(-2, -1)))
    coeff = 24.0 * strength * (2.0 * cubed * cubed - cubed) * ratio / reach_sq
    force = lax.optimization_barrier(jnp.sum(coeff[None] * delta, axis=-1))
    return (force, energy)

def reference(coords, ref_coords, restraint, atom_types, well_table, radius_table, tile_lists, halo_index):
    depth_atom = well_table[atom_types]
    radius_atom = radius_table[atom_types]
    tiles_dev = ATOMS_DEV // TILE
    pick_atoms = jax.vmap(lambda source, index: source[:, index])
    pick_tiles = jax.vmap(lambda source, index: source[:, index, :])

    def one_image(inputs):
        position, lists, halos = inputs
        feats = jnp.concatenate([position, depth_atom[None], radius_atom[None]], axis=0)
        slabs = feats.reshape(5, N_SPACE, ATOMS_DEV).transpose(1, 0, 2)
        zero_slab = jnp.zeros((1, 5, ATOMS_DEV), jnp.float32)
        below = jnp.concatenate([zero_slab, slabs[:-1]], axis=0)
        above = jnp.concatenate([slabs[1:], zero_slab], axis=0)
        wanted = halos.reshape(2, N_SPACE, HALO)
        lower = pick_atoms(below, wanted[0])
        upper = pick_atoms(above, wanted[1])
        extended = jnp.concatenate([slabs, lower, upper], axis=2).reshape(N_SPACE, 5, -1, TILE)
        own = slabs.reshape(N_SPACE, 5, tiles_dev, TILE).transpose(1, 0, 2, 3)
        chosen = lists.reshape(PARTNERS, N_SPACE, tiles_dev)

        def add_partner(carry, index):
            partner = pick_tiles(extended, index).transpose(1, 0, 2, 3)
            force, energy = pair_terms(own, partner)
            return ((carry[0] + force, carry[1] + jnp.sum(energy)), None)
        start = (jnp.zeros((3, N_SPACE, tiles_dev, TILE), jnp.float32), jnp.zeros((), jnp.float32))
        (force, energy), _ = lax.scan(add_partner, start, chosen)
        force = force.reshape(3, ATOMS)
        offset = position - ref_coords
        force = force - restraint[None] * offset
        energy = (0.5 * energy + 0.5 * jnp.sum(restraint[None] * offset * offset)) / ATOMS
        return (force, energy)
    forces, energies = lax.map(one_image, (coords, tile_lists, halo_index))
    zero_image = jnp.zeros((1, 3, ATOMS), jnp.float32)
    before = jnp.concatenate([zero_image, coords[:-1]], axis=0)
    after = jnp.concatenate([coords[1:], zero_image], axis=0)
    ahead = after - coords
    behind = coords - before
    ahead_len = jnp.sqrt(lax.optimization_barrier(jnp.sum(ahead * ahead, axis=(1, 2))) + small_eps)[:, None, None]
    behind_len = jnp.sqrt(lax.optimization_barrier(jnp.sum(behind * behind, axis=(1, 2))) + small_eps)[:, None, None]
    tangent = ahead / ahead_len + behind / behind_len
    tan_len = jnp.sqrt(lax.optimization_barrier(jnp.sum(tangent * tangent, axis=(1, 2))) + small_eps)[:, None, None]
    unit = tangent / tan_len
    along = lax.optimization_barrier(jnp.sum(forces * unit, axis=(1, 2)))[:, None, None]
    banded = forces - along * unit + spring_k * (ahead_len - behind_len) * unit
    order = jnp.arange(IMAGES, dtype=jnp.int32)[:, None, None]
    ends = (order == 0) | (order == IMAGES - 1)
    neb_force = jnp.where(ends, forces, banded)
    return (neb_force, energies)
```

```python
import jax
import jax.numpy as jnp
from jax import lax
from jax.experimental import pallas as pl
from jax.experimental.pallas import tpu as pltpu
from jax.sharding import PartitionSpec as P

TILE = 128
PARTNERS = 4

soft_core = 1.0
spring_k = 2.0
small_eps = 1e-06


def lookup(row, index):
    return jnp.take_along_axis(
        jnp.broadcast_to(row, index.shape), index, axis=1, mode="promise_in_bounds"
    )


def pair_kernel(
    lists_ref, edge_ref, coords_ref, types_ref, low_ref, low_types_ref, up_ref, up_types_ref,
    halo_ref, table_ref, force_ref, energy_ref, param_ref, feat_ref, cols_ref,
):
    images = coords_ref.shape[0]
    tiles = coords_ref.shape[2] // TILE
    halo_tiles = halo_ref.shape[2]
    wells, radii = table_ref[0:1, :], table_ref[1:2, :]
    for b in range(tiles // 8):
        kinds = types_ref[b * 8:(b + 1) * 8, :]
        param_ref[0, b * 8:(b + 1) * 8, :] = lookup(wells, kinds)
        param_ref[1, b * 8:(b + 1) * 8, :] = lookup(radii, kinds)

    for m in range(images):
        for t in range(tiles):
            feat_ref[m, t, 0:3, :] = coords_ref[m, :, t * TILE:(t + 1) * TILE]
            feat_ref[m, t, 3:4, :] = param_ref[0, t:t + 1, :]
            feat_ref[m, t, 4:5, :] = param_ref[1, t:t + 1, :]
        for side, (src, kinds) in enumerate(((low_ref, low_types_ref), (up_ref, up_types_ref))):
            index = halo_ref[m, side]
            lane = jnp.bitwise_and(index, TILE - 1)
            row = jnp.right_shift(index, 7)
            x = jnp.zeros((halo_tiles, TILE), jnp.float32)
            got = [x, x, x, jnp.zeros((halo_tiles, TILE), jnp.int32)]
            for t in range(tiles):
                hit = row == t
                for f in range(3):
                    g = lookup(src[m, f:f + 1, t * TILE:(t + 1) * TILE], lane)
                    got[f] = jnp.where(hit, g, got[f])
                got[3] = jnp.where(hit, lookup(kinds[t:t + 1, :], lane), got[3])
            inside = jnp.full((halo_tiles, TILE), edge_ref[side]) > 0
            full = got[:3] + [lookup(wells, got[3]), lookup(radii, got[3])]
            for f in range(5):
                value = jnp.where(inside, full[f], 0.0)
                for u in range(halo_tiles):
                    feat_ref[m, tiles + side * halo_tiles + u, f:f + 1, :] = value[u:u + 1, :]

    ext = tiles + 2 * halo_tiles

    def turn(n, carry):
        for m in range(images):
            cols_ref[m, n, :, 0:8] = feat_ref[m, n].T
        return carry

    lax.fori_loop(0, ext, turn, 0)

    for m in range(images):
        def tile_step(t, energy):
            own = [jnp.broadcast_to(feat_ref[m, t, f:f + 1, :], (8, TILE)) for f in range(5)]
            zero = jnp.zeros((8, TILE), jnp.float32)
            fx, fy, fz, en = zero, zero, zero, zero
            for k in range(PARTNERS):
                p = lists_ref[m, k, t]
                for j in range(TILE // 8):
                    v = cols_ref[m, p, j * 8:(j + 1) * 8, 0:8]
                    part = [jnp.broadcast_to(v[:, f:f + 1], (8, TILE)) for f in range(5)]
                    dx, dy, dz = own[0] - part[0], own[1] - part[1], own[2] - part[2]
                    reach = own[4] + part[4]
                    reach_sq = reach * reach
                    den = (dx * dx + dy * dy) + (dz * dz + reach_sq)
                    inv = pl.reciprocal(den, approx=True)
                    inv = inv * (2.0 - den * inv)
                    ratio = reach_sq * inv
                    cubed = ratio * ratio * ratio
                    a = part[3] * cubed
                    b = a * cubed
                    e = b - a
                    en = en + e
                    c = (b + e) * inv
                    fx = fx + c * dx
                    fy = fy + c * dy
                    fz = fz + c * dz
            scale = 24.0 * feat_ref[m, t, 3:4, :]
            rows = jnp.concatenate(
                [jnp.sum(f, axis=0, keepdims=True) * scale for f in (fx, fy, fz)], axis=0
            )
            force_ref[m, :, pl.ds(pl.multiple_of(t * TILE, TILE), TILE)] = rows
            return energy + 4.0 * own[3] * en

        energy_ref[m] = lax.fori_loop(0, tiles, tile_step, jnp.zeros((8, TILE), jnp.float32))


def pair_forces(lists, edge, coords, types, low, low_types, up, up_types, halo, table):
    images, _, atoms = coords.shape
    tiles = atoms // TILE
    ext = tiles + 2 * halo.shape[2]
    vmem = pl.BlockSpec(memory_space=pltpu.VMEM)
    smem = pl.BlockSpec(memory_space=pltpu.SMEM)
    return pl.pallas_call(
        pair_kernel,
        out_shape=(
            jax.ShapeDtypeStruct((images, 3, atoms), jnp.float32),
            jax.ShapeDtypeStruct((images, 8, TILE), jnp.float32),
        ),
        in_specs=[smem, smem] + [vmem] * 8,
        out_specs=(vmem, vmem),
        scratch_shapes=[
            pltpu.VMEM((2, tiles, TILE), jnp.float32),
            pltpu.VMEM((images, ext, 8, TILE), jnp.float32),
            pltpu.VMEM((images, ext, TILE, TILE), jnp.float32),
        ],
        compiler_params=pltpu.CompilerParams(vmem_limit_bytes=40 * 1024 * 1024),
    )(lists, edge, coords, types, low, low_types, up, up_types, halo, table)


def image_total(values):
    return jnp.sum(values, axis=(1, 2))


def body(
    coords, ref_coords, restraint, atom_types, well_table, radius_table, tile_lists, halo_index
):
    img_local, _, atoms_local = coords.shape
    tiles_local = atoms_local // TILE
    n_space = lax.axis_size("space")
    n_image = lax.axis_size("image")
    types = atom_types.reshape(tiles_local, TILE)
    table = jnp.pad(
        jnp.stack([well_table, radius_table]), ((0, 0), (0, TILE - well_table.shape[0]))
    )
    up = [(i, i + 1) for i in range(n_space - 1)]
    down = [(j, i) for i, j in up]
    low = lax.ppermute(coords, "space", up)
    high = lax.ppermute(coords, "space", down)
    low_types = lax.ppermute(types, "space", up)
    high_types = lax.ppermute(types, "space", down)
    up_i = [(i, i + 1) for i in range(n_image - 1)]
    down_i = [(j, i) for i, j in up_i]
    before = lax.ppermute(coords[-1:], "image", up_i)
    after = lax.ppermute(coords[:1], "image", down_i)
    slab = lax.axis_index("space")
    edge = jnp.stack([slab > 0, slab < n_space - 1]).astype(jnp.int32)
    halo = halo_index.reshape(img_local, 2, -1, TILE)
    pair_force, pair_energy = pair_forces(
        tile_lists, edge, coords, types, low, low_types, high, high_types, halo, table
    )
    offset = coords - ref_coords[None]
    forces = pair_force - restraint[None, None] * offset
    local_energy = 0.5 * image_total(pair_energy) + 0.5 * image_total(
        restraint[None, None] * offset * offset
    )
    rims = jnp.concatenate([before, coords, after], axis=0)
    ahead = rims[2:] - coords
    behind = coords - rims[:-2]
    ahead_sq, behind_sq, cross, force_ahead, force_behind, energy_sum = lax.psum(
        (
            image_total(ahead * ahead),
            image_total(behind * behind),
            image_total(ahead * behind),
            image_total(forces * ahead),
            image_total(forces * behind),
            local_energy,
        ),
        "space",
    )
    ahead_norm = jnp.sqrt(ahead_sq + small_eps)
    behind_norm = jnp.sqrt(behind_sq + small_eps)
    tan_sq = (
        ahead_sq / (ahead_norm * ahead_norm)
        + 2.0 * cross / (ahead_norm * behind_norm)
        + behind_sq / (behind_norm * behind_norm)
    )
    tan_norm = jnp.sqrt(tan_sq + small_eps)
    ahead_len = ahead_norm[:, None, None]
    behind_len = behind_norm[:, None, None]
    tan_len = tan_norm[:, None, None]
    unit = (ahead / ahead_len + behind / behind_len) / tan_len
    along = ((force_ahead / ahead_norm + force_behind / behind_norm) / tan_norm)[:, None, None]
    banded = forces - along * unit + spring_k * (ahead_len - behind_len) * unit
    total_images = img_local * n_image
    order = lax.axis_index("image") * img_local + jnp.arange(img_local, dtype=jnp.int32)
    ends = ((order == 0) | (order == total_images - 1))[:, None, None]
    neb_force = jnp.where(ends, forces, banded)
    energies = energy_sum / (atoms_local * n_space)
    return (neb_force, energies)


def solution(mesh):
    in_specs = (
        P("image", None, "space"),
        P(None, "space"),
        P("space"),
        P("space"),
        P(),
        P(),
        P("image", None, "space"),
        P("image", None, "space"),
    )
    out_specs = (P("image", None, "space"), P("image"))
    return jax.shard_map(body, mesh=mesh, in_specs=in_specs, out_specs=out_specs, check_vma=False)
```

```python
import functools

import jax
import jax.numpy as jnp
from jax import lax
from jax.experimental import pallas as pl
from jax.experimental.pallas import tpu as pltpu
from jax.sharding import PartitionSpec as P

TILE = 128
PARTNERS = 4

soft_core = 1.0
spring_k = 2.0
small_eps = 1e-06


def lookup(row, index):
    return jnp.take_along_axis(
        jnp.broadcast_to(row, index.shape), index, axis=1, mode="promise_in_bounds"
    )


def pair_kernel(
    lists_ref, edge_ref, coords_ref, types_ref, low_ref, low_types_ref, up_ref, up_types_ref,
    halo_ref, table_ref, force_ref, energy_ref, param_ref, feat_ref, sums_ref,
):
    images = coords_ref.shape[0]
    tiles = coords_ref.shape[2]
    halo_tiles = halo_ref.shape[2]
    wells, radii = table_ref[0:1, :], table_ref[1:2, :]
    for b in range(tiles // 8):
        kinds = types_ref[b * 8:(b + 1) * 8, :]
        param_ref[0, b * 8:(b + 1) * 8, :] = lookup(wells, kinds)
        param_ref[1, b * 8:(b + 1) * 8, :] = lookup(radii, kinds)

    for m in range(images):
        for t in range(tiles):
            for f in range(3):
                feat_ref[m, t, f:f + 1, :] = coords_ref[m, f, t:t + 1, :]
            feat_ref[m, t, 3:4, :] = param_ref[0, t:t + 1, :]
            feat_ref[m, t, 4:5, :] = param_ref[1, t:t + 1, :]
        for side, (src, kinds) in enumerate(((low_ref, low_types_ref), (up_ref, up_types_ref))):
            index = halo_ref[m, side]
            lane = jnp.bitwise_and(index, TILE - 1)
            row = jnp.right_shift(index, 7)
            x = jnp.zeros((halo_tiles, TILE), jnp.float32)
            got = [x, x, x, jnp.zeros((halo_tiles, TILE), jnp.int32)]
            for t in range(tiles):
                hit = row == t
                for f in range(3):
                    g = lookup(src[m, f, t:t + 1, :], lane)
                    got[f] = jnp.where(hit, g, got[f])
                got[3] = jnp.where(hit, lookup(kinds[t:t + 1, :], lane), got[3])
            inside = jnp.full((halo_tiles, TILE), edge_ref[side]) > 0
            full = got[:3] + [lookup(wells, got[3]), lookup(radii, got[3])]
            for f in range(5):
                value = jnp.where(inside, full[f], 0.0)
                for u in range(halo_tiles):
                    feat_ref[m, tiles + side * halo_tiles + u, f:f + 1, :] = value[u:u + 1, :]

    sums_ref[...] = jnp.zeros_like(sums_ref)
    for m in range(images):
        def tile_step(t, energy):
            turned = feat_ref[m, t].T
            picks = [lists_ref[m, k, t] for k in range(PARTNERS)]
            for i in range(TILE // 8):
                rows = slice(i * 8, (i + 1) * 8)
                own = [jnp.broadcast_to(turned[rows, f:f + 1], (8, TILE)) for f in range(5)]
                zero = jnp.zeros((8, TILE), jnp.float32)
                fx, fy, fz, en = zero, zero, zero, zero
                for p in picks:
                    part = [
                        jnp.broadcast_to(feat_ref[m, p, f:f + 1, :], (8, TILE)) for f in range(5)
                    ]
                    dx, dy, dz = own[0] - part[0], own[1] - part[1], own[2] - part[2]
                    reach = own[4] + part[4]
                    reach_sq = reach * reach
                    den = (dx * dx + dy * dy) + (dz * dz + reach_sq)
                    inv = pltpu.reciprocal(den, approx=True)
                    ratio = reach_sq * inv
                    cubed = ratio * ratio * ratio
                    a = part[3] * cubed
                    b = a * cubed
                    e = b - a
                    en = en + e
                    c = (b + e) * inv
                    fx = fx + c * dx
                    fy = fy + c * dy
                    fz = fz + c * dz
                energy = energy + own[3] * en
                for f, value in enumerate((fx, fy, fz)):
                    sums_ref[rows, f:f + 1] = jnp.sum(value, axis=1, keepdims=True)
            out = (24.0 * feat_ref[m, t, 3:4, :]) * sums_ref[...].T[0:3, :]
            force_ref[m, :, pl.ds(pl.multiple_of(t * TILE, TILE), TILE)] = out
            return energy

        energy_ref[m] = 4.0 * lax.fori_loop(
            0, tiles, tile_step, jnp.zeros((8, TILE), jnp.float32)
        )


def exchange_kernel(
    n_space, n_image, coords_ref, types_ref, low_ref, low_types_ref, up_ref, up_types_ref,
    before_ref, after_ref, send_sem, recv_sem,
):
    slab, image = lax.axis_index("space"), lax.axis_index("image")
    last = coords_ref.shape[0] - 1
    links = (
        (slab < n_space - 1, slab > 0, "space", slab, 1,
         ((coords_ref, low_ref), (types_ref, low_types_ref))),
        (slab > 0, slab < n_space - 1, "space", slab, -1,
         ((coords_ref, up_ref), (types_ref, up_types_ref))),
        (image < n_image - 1, image > 0, "image", image, 1,
         ((coords_ref.at[pl.ds(last, 1)], before_ref),)),
        (image > 0, image < n_image - 1, "image", image, -1,
         ((coords_ref.at[pl.ds(0, 1)], after_ref),)),
    )
    barrier = pltpu.get_barrier_semaphore()
    for sends, _, axis, here, step, _ in links:
        @pl.when(sends)
        def _(axis=axis, here=here, step=step):
            pl.semaphore_signal(
                barrier, inc=1, device_id={axis: here + step}, device_id_type=pl.DeviceIdType.MESH
            )
    peers = sum(link[0].astype(jnp.int32) for link in links)
    pl.semaphore_wait(barrier, peers)

    slot = 0
    waits = []
    for sends, gets, axis, here, step, pairs in links:
        copies = []
        for src, dst in pairs:
            copies.append(pltpu.make_async_remote_copy(
                src_ref=src, dst_ref=dst, send_sem=send_sem.at[slot], recv_sem=recv_sem.at[slot],
                device_id={axis: here + step}, device_id_type=pl.DeviceIdType.MESH,
            ))
            slot += 1
        @pl.when(sends)
        def _(copies=copies):
            for c in copies:
                c.start()
        @pl.when(jnp.logical_not(gets))
        def _(pairs=pairs):
            for _, dst in pairs:
                dst[...] = jnp.zeros_like(dst)
        waits.append((sends, gets, copies))
    for sends, gets, copies in waits:
        @pl.when(gets)
        def _(copies=copies):
            for c in copies:
                c.wait_recv()
    for sends, gets, copies in waits:
        @pl.when(sends)
        def _(copies=copies):
            for c in copies:
                c.wait_send()


def exchange(coords, types, n_space, n_image):
    vmem = pl.BlockSpec(memory_space=pltpu.VMEM)
    whole = jax.ShapeDtypeStruct(coords.shape, coords.dtype)
    kinds = jax.ShapeDtypeStruct(types.shape, types.dtype)
    rim = jax.ShapeDtypeStruct((1,) + coords.shape[1:], coords.dtype)
    return pl.pallas_call(
        functools.partial(exchange_kernel, n_space, n_image),
        out_shape=(whole, kinds, whole, kinds, rim, rim),
        in_specs=[vmem, vmem],
        out_specs=(vmem,) * 6,
        scratch_shapes=[pltpu.SemaphoreType.DMA((6,)), pltpu.SemaphoreType.DMA((6,))],
        compiler_params=pltpu.CompilerParams(collective_id=0, has_side_effects=True),
    )(coords, types)


def pair_forces(lists, edge, coords, types, low, low_types, up, up_types, halo, table):
    images, _, tiles, _ = coords.shape
    atoms = tiles * TILE
    ext = tiles + 2 * halo.shape[2]
    vmem = pl.BlockSpec(memory_space=pltpu.VMEM)
    smem = pl.BlockSpec(memory_space=pltpu.SMEM)
    return pl.pallas_call(
        pair_kernel,
        out_shape=(
            jax.ShapeDtypeStruct((images, 3, atoms), jnp.float32),
            jax.ShapeDtypeStruct((images, 8, TILE), jnp.float32),
        ),
        in_specs=[smem, smem] + [vmem] * 8,
        out_specs=(vmem, vmem),
        scratch_shapes=[
            pltpu.VMEM((2, tiles, TILE), jnp.float32),
            pltpu.VMEM((images, ext, 8, TILE), jnp.float32),
            pltpu.VMEM((TILE, 8), jnp.float32),
        ],
        compiler_params=pltpu.CompilerParams(vmem_limit_bytes=40 * 1024 * 1024),
    )(lists, edge, coords, types, low, low_types, up, up_types, halo, table)


def image_total(values):
    return jnp.sum(values, axis=(1, 2))


def body(
    coords, ref_coords, restraint, atom_types, well_table, radius_table, tile_lists, halo_index
):
    img_local, _, atoms_local = coords.shape
    tiles_local = atoms_local // TILE
    n_space = lax.axis_size("space")
    n_image = lax.axis_size("image")
    types = atom_types.reshape(tiles_local, TILE)
    table = jnp.pad(
        jnp.stack([well_table, radius_table]), ((0, 0), (0, TILE - well_table.shape[0]))
    )
    tiled = coords.reshape(img_local, 3, tiles_local, TILE)
    low, low_types, high, high_types, before, after = exchange(tiled, types, n_space, n_image)
    before = before.reshape(1, 3, atoms_local)
    after = after.reshape(1, 3, atoms_local)
    slab = lax.axis_index("space")
    edge = jnp.stack([slab > 0, slab < n_space - 1]).astype(jnp.int32)
    halo = halo_index.reshape(img_local, 2, -1, TILE)
    pair_force, pair_energy = pair_forces(
        tile_lists, edge, tiled, types, low, low_types, high, high_types, halo, table
    )
    offset = coords - ref_coords[None]
    forces = pair_force - restraint[None, None] * offset
    local_energy = 0.5 * image_total(pair_energy) + 0.5 * image_total(
        restraint[None, None] * offset * offset
    )
    rims = jnp.concatenate([before, coords, after], axis=0)
    ahead = rims[2:] - coords
    behind = coords - rims[:-2]
    ahead_sq, behind_sq, cross, force_ahead, force_behind, energy_sum = lax.psum(
        (
            image_total(ahead * ahead),
            image_total(behind * behind),
            image_total(ahead * behind),
            image_total(forces * ahead),
            image_total(forces * behind),
            local_energy,
        ),
        "space",
    )
    ahead_norm = jnp.sqrt(ahead_sq + small_eps)
    behind_norm = jnp.sqrt(behind_sq + small_eps)
    tan_sq = (
        ahead_sq / (ahead_norm * ahead_norm)
        + 2.0 * cross / (ahead_norm * behind_norm)
        + behind_sq / (behind_norm * behind_norm)
    )
    tan_norm = jnp.sqrt(tan_sq + small_eps)
    ahead_len = ahead_norm[:, None, None]
    behind_len = behind_norm[:, None, None]
    tan_len = tan_norm[:, None, None]
    unit = (ahead / ahead_len + behind / behind_len) / tan_len
    along = ((force_ahead / ahead_norm + force_behind / behind_norm) / tan_norm)[:, None, None]
    banded = forces - along * unit + spring_k * (ahead_len - behind_len) * unit
    total_images = img_local * n_image
    order = lax.axis_index("image") * img_local + jnp.arange(img_local, dtype=jnp.int32)
    ends = ((order == 0) | (order == total_images - 1))[:, None, None]
    neb_force = jnp.where(ends, forces, banded)
    energies = energy_sum / (atoms_local * n_space)
    return (neb_force, energies)


def solution(mesh):
    in_specs = (
        P("image", None, "space"),
        P(None, "space"),
        P("space"),
        P("space"),
        P(),
        P(),
        P("image", None, "space"),
        P("image", None, "space"),
    )
    out_specs = (P("image", None, "space"), P("image"))
    return jax.shard_map(body, mesh=mesh, in_specs=in_specs, out_specs=out_specs, check_vma=False)
```

```python
import functools

import jax
import jax.numpy as jnp
from jax import lax
from jax.experimental import pallas as pl
from jax.experimental.pallas import tpu as pltpu
from jax.sharding import PartitionSpec as P

TILE = 128
PARTNERS = 4

soft_core = 1.0
spring_k = 2.0
small_eps = 1e-06


def lookup(row, index):
    return jnp.take_along_axis(
        jnp.broadcast_to(row, index.shape), index, axis=1, mode="promise_in_bounds"
    )


def pair_kernel(
    lists_ref, edge_ref, coords_ref, types_ref, low_ref, low_types_ref, up_ref, up_types_ref,
    halo_ref, table_ref, force_ref, energy_ref, param_ref, feat_ref, cols_ref,
):
    images = coords_ref.shape[0]
    tiles = coords_ref.shape[2]
    halo_tiles = halo_ref.shape[2]
    wells, radii = table_ref[0:1, :], table_ref[1:2, :]
    for b in range(tiles // 8):
        kinds = types_ref[b * 8:(b + 1) * 8, :]
        param_ref[0, b * 8:(b + 1) * 8, :] = lookup(wells, kinds)
        param_ref[1, b * 8:(b + 1) * 8, :] = lookup(radii, kinds)

    for m in range(images):
        for t in range(tiles):
            for f in range(3):
                feat_ref[m, t, f:f + 1, :] = coords_ref[m, f, t:t + 1, :]
            feat_ref[m, t, 3:4, :] = param_ref[0, t:t + 1, :]
            feat_ref[m, t, 4:5, :] = param_ref[1, t:t + 1, :]
        for side, (src, kinds) in enumerate(((low_ref, low_types_ref), (up_ref, up_types_ref))):
            index = halo_ref[m, side]
            lane = jnp.bitwise_and(index, TILE - 1)
            row = jnp.right_shift(index, 7)
            x = jnp.zeros((halo_tiles, TILE), jnp.float32)
            got = [x, x, x, jnp.zeros((halo_tiles, TILE), jnp.int32)]
            for t in range(tiles):
                hit = row == t
                for f in range(3):
                    g = lookup(src[m, f, t:t + 1, :], lane)
                    got[f] = jnp.where(hit, g, got[f])
                got[3] = jnp.where(hit, lookup(kinds[t:t + 1, :], lane), got[3])
            inside = jnp.full((halo_tiles, TILE), edge_ref[side]) > 0
            full = got[:3] + [lookup(wells, got[3]), lookup(radii, got[3])]
            for f in range(5):
                value = jnp.where(inside, full[f], 0.0)
                for u in range(halo_tiles):
                    feat_ref[m, tiles + side * halo_tiles + u, f:f + 1, :] = value[u:u + 1, :]

    ext = tiles + 2 * halo_tiles
    for m in range(images):
        def spread(n, carry):
            turned = feat_ref[m, n].T
            for f in range(5):
                cols_ref[f, n] = jnp.broadcast_to(turned[:, f:f + 1], (TILE, TILE))
            return carry

        lax.fori_loop(0, ext, spread, 0)

        def tile_step(t, energy):
            own = [jnp.broadcast_to(feat_ref[m, t, f:f + 1, :], (8, TILE)) for f in range(5)]
            zero = jnp.zeros((8, TILE), jnp.float32)
            fx, fy, fz, en = zero, zero, zero, zero
            for k in range(PARTNERS):
                p = lists_ref[m, k, t]
                for j in range(TILE // 8):
                    part = [cols_ref[f, p, j * 8:(j + 1) * 8, :] for f in range(5)]
                    dx, dy, dz = own[0] - part[0], own[1] - part[1], own[2] - part[2]
                    reach = own[4] + part[4]
                    reach_sq = reach * reach
                    den = (dx * dx + dy * dy) + (dz * dz + reach_sq)
                    inv = pltpu.reciprocal(den, approx=True)
                    ratio = reach_sq * inv
                    cubed = ratio * ratio * ratio
                    a = part[3] * cubed
                    b = a * cubed
                    e = b - a
                    en = en + e
                    c = (b + e) * inv
                    fx = fx + c * dx
                    fy = fy + c * dy
                    fz = fz + c * dz
            scale = 24.0 * feat_ref[m, t, 3:4, :]
            force_ref[m, :, pl.ds(pl.multiple_of(t * TILE, TILE), TILE)] = jnp.concatenate(
                [jnp.sum(f, axis=0, keepdims=True) * scale for f in (fx, fy, fz)], axis=0
            )
            return energy + 4.0 * own[3] * en

        energy_ref[m] = lax.fori_loop(0, tiles, tile_step, jnp.zeros((8, TILE), jnp.float32))


def exchange_kernel(
    n_space, n_image, coords_ref, types_ref, low_ref, low_types_ref, up_ref, up_types_ref,
    before_ref, after_ref, send_sem, recv_sem,
):
    slab, image = lax.axis_index("space"), lax.axis_index("image")
    last = coords_ref.shape[0] - 1
    links = (
        (slab < n_space - 1, slab > 0, "space", slab, 1,
         ((coords_ref, low_ref), (types_ref, low_types_ref))),
        (slab > 0, slab < n_space - 1, "space", slab, -1,
         ((coords_ref, up_ref), (types_ref, up_types_ref))),
        (image < n_image - 1, image > 0, "image", image, 1,
         ((coords_ref.at[pl.ds(last, 1)], before_ref),)),
        (image > 0, image < n_image - 1, "image", image, -1,
         ((coords_ref.at[pl.ds(0, 1)], after_ref),)),
    )
    barrier = pltpu.get_barrier_semaphore()
    for sends, _, axis, here, step, _ in links:
        @pl.when(sends)
        def _(axis=axis, here=here, step=step):
            pl.semaphore_signal(
                barrier, inc=1, device_id={axis: here + step}, device_id_type=pl.DeviceIdType.MESH
            )
    peers = sum(link[0].astype(jnp.int32) for link in links)
    pl.semaphore_wait(barrier, peers)

    slot = 0
    waits = []
    for sends, gets, axis, here, step, pairs in links:
        copies = []
        for src, dst in pairs:
            copies.append(pltpu.make_async_remote_copy(
                src_ref=src, dst_ref=dst, send_sem=send_sem.at[slot], recv_sem=recv_sem.at[slot],
                device_id={axis: here + step}, device_id_type=pl.DeviceIdType.MESH,
            ))
            slot += 1
        @pl.when(sends)
        def _(copies=copies):
            for c in copies:
                c.start()
        @pl.when(jnp.logical_not(gets))
        def _(pairs=pairs):
            for _, dst in pairs:
                dst[...] = jnp.zeros_like(dst)
        waits.append((sends, gets, copies))
    for sends, gets, copies in waits:
        @pl.when(gets)
        def _(copies=copies):
            for c in copies:
                c.wait_recv()
    for sends, gets, copies in waits:
        @pl.when(sends)
        def _(copies=copies):
            for c in copies:
                c.wait_send()


def exchange(coords, types, n_space, n_image):
    vmem = pl.BlockSpec(memory_space=pltpu.VMEM)
    whole = jax.ShapeDtypeStruct(coords.shape, coords.dtype)
    kinds = jax.ShapeDtypeStruct(types.shape, types.dtype)
    rim = jax.ShapeDtypeStruct((1,) + coords.shape[1:], coords.dtype)
    return pl.pallas_call(
        functools.partial(exchange_kernel, n_space, n_image),
        out_shape=(whole, kinds, whole, kinds, rim, rim),
        in_specs=[vmem, vmem],
        out_specs=(vmem,) * 6,
        scratch_shapes=[pltpu.SemaphoreType.DMA((6,)), pltpu.SemaphoreType.DMA((6,))],
        compiler_params=pltpu.CompilerParams(collective_id=0, has_side_effects=True),
    )(coords, types)


def pair_forces(lists, edge, coords, types, low, low_types, up, up_types, halo, table):
    images, _, tiles, _ = coords.shape
    atoms = tiles * TILE
    ext = tiles + 2 * halo.shape[2]
    vmem = pl.BlockSpec(memory_space=pltpu.VMEM)
    smem = pl.BlockSpec(memory_space=pltpu.SMEM)
    return pl.pallas_call(
        pair_kernel,
        out_shape=(
            jax.ShapeDtypeStruct((images, 3, atoms), jnp.float32),
            jax.ShapeDtypeStruct((images, 8, TILE), jnp.float32),
        ),
        in_specs=[smem, smem] + [vmem] * 8,
        out_specs=(vmem, vmem),
        scratch_shapes=[
            pltpu.VMEM((2, tiles, TILE), jnp.float32),
            pltpu.VMEM((images, ext, 8, TILE), jnp.float32),
            pltpu.VMEM((5, ext, TILE, TILE), jnp.float32),
        ],
        compiler_params=pltpu.CompilerParams(vmem_limit_bytes=40 * 1024 * 1024),
    )(lists, edge, coords, types, low, low_types, up, up_types, halo, table)


def image_total(values):
    return jnp.sum(values, axis=(1, 2))


def body(
    coords, ref_coords, restraint, atom_types, well_table, radius_table, tile_lists, halo_index
):
    img_local, _, atoms_local = coords.shape
    tiles_local = atoms_local // TILE
    n_space = lax.axis_size("space")
    n_image = lax.axis_size("image")
    types = atom_types.reshape(tiles_local, TILE)
    table = jnp.pad(
        jnp.stack([well_table, radius_table]), ((0, 0), (0, TILE - well_table.shape[0]))
    )
    tiled = coords.reshape(img_local, 3, tiles_local, TILE)
    low, low_types, high, high_types, before, after = exchange(tiled, types, n_space, n_image)
    before = before.reshape(1, 3, atoms_local)
    after = after.reshape(1, 3, atoms_local)
    slab = lax.axis_index("space")
    edge = jnp.stack([slab > 0, slab < n_space - 1]).astype(jnp.int32)
    halo = halo_index.reshape(img_local, 2, -1, TILE)
    pair_force, pair_energy = pair_forces(
        tile_lists, edge, tiled, types, low, low_types, high, high_types, halo, table
    )
    offset = coords - ref_coords[None]
    forces = pair_force - restraint[None, None] * offset
    local_energy = 0.5 * image_total(pair_energy) + 0.5 * image_total(
        restraint[None, None] * offset * offset
    )
    rims = jnp.concatenate([before, coords, after], axis=0)
    ahead = rims[2:] - coords
    behind = coords - rims[:-2]
    ahead_sq, behind_sq, cross, force_ahead, force_behind, energy_sum = lax.psum(
        (
            image_total(ahead * ahead),
            image_total(behind * behind),
            image_total(ahead * behind),
            image_total(forces * ahead),
            image_total(forces * behind),
            local_energy,
        ),
        "space",
    )
    ahead_norm = jnp.sqrt(ahead_sq + small_eps)
    behind_norm = jnp.sqrt(behind_sq + small_eps)
    tan_sq = (
        ahead_sq / (ahead_norm * ahead_norm)
        + 2.0 * cross / (ahead_norm * behind_norm)
        + behind_sq / (behind_norm * behind_norm)
    )
    tan_norm = jnp.sqrt(tan_sq + small_eps)
    ahead_len = ahead_norm[:, None, None]
    behind_len = behind_norm[:, None, None]
    tan_len = tan_norm[:, None, None]
    unit = (ahead / ahead_len + behind / behind_len) / tan_len
    along = ((force_ahead / ahead_norm + force_behind / behind_norm) / tan_norm)[:, None, None]
    banded = forces - along * unit + spring_k * (ahead_len - behind_len) * unit
    total_images = img_local * n_image
    order = lax.axis_index("image") * img_local + jnp.arange(img_local, dtype=jnp.int32)
    ends = ((order == 0) | (order == total_images - 1))[:, None, None]
    neb_force = jnp.where(ends, forces, banded)
    energies = energy_sum / (atoms_local * n_space)
    return (neb_force, energies)


def solution(mesh):
    in_specs = (
        P("image", None, "space"),
        P(None, "space"),
        P("space"),
        P("space"),
        P(),
        P(),
        P("image", None, "space"),
        P("image", None, "space"),
    )
    out_specs = (P("image", None, "space"), P("image"))
    return jax.shard_map(body, mesh=mesh, in_specs=in_specs, out_specs=out_specs, check_vma=False)
```

```python
import functools

import jax
import jax.numpy as jnp
from jax import lax
from jax.experimental import pallas as pl
from jax.experimental.pallas import tpu as pltpu
from jax.sharding import PartitionSpec as P

TILE = 128
PARTNERS = 4

soft_core = 1.0
spring_k = 2.0
small_eps = 1e-06


def lookup(row, index):
    return jnp.take_along_axis(
        jnp.broadcast_to(row, index.shape), index, axis=1, mode="promise_in_bounds"
    )


def pair_kernel(
    lists_ref, edge_ref, coords_ref, types_ref, low_ref, low_types_ref, up_ref, up_types_ref,
    halo_ref, table_ref, force_ref, energy_ref, param_ref, feat_ref, cols_ref,
):
    images = coords_ref.shape[0]
    tiles = coords_ref.shape[2]
    halo_tiles = halo_ref.shape[2] // TILE
    wells, radii = table_ref[0:1, :], table_ref[1:2, :]
    for b in range(tiles // 8):
        kinds = types_ref[b * 8:(b + 1) * 8, :]
        param_ref[0, b * 8:(b + 1) * 8, :] = lookup(wells, kinds)
        param_ref[1, b * 8:(b + 1) * 8, :] = lookup(radii, kinds)

    for m in range(images):
        for t in range(tiles):
            for f in range(3):
                feat_ref[m, t, f:f + 1, :] = coords_ref[m, f, t:t + 1, :]
            feat_ref[m, t, 3:4, :] = param_ref[0, t:t + 1, :]
            feat_ref[m, t, 4:5, :] = param_ref[1, t:t + 1, :]
        for side, (src, kinds) in enumerate(((low_ref, low_types_ref), (up_ref, up_types_ref))):
            index = halo_ref[m, side:side + 1, :]
            lane = jnp.bitwise_and(index, TILE - 1)
            row = jnp.right_shift(index, 7)
            width = index.shape[1]
            pick = lax.broadcasted_iota(jnp.int32, (TILE, width), 0) == lane
            pick = jnp.where(pick, 1.0, 0.0).astype(jnp.bfloat16)
            hit = lax.broadcasted_iota(jnp.int32, (tiles, width), 0) == row

            def choose(piece):
                found = jnp.dot(piece, pick, preferred_element_type=jnp.float32)
                return jnp.sum(jnp.where(hit, found, 0.0), axis=0, keepdims=True)

            got = []
            for f in range(3):
                x = src[m, f]
                high = x.astype(jnp.bfloat16)
                rest = x - high.astype(jnp.float32)
                mid = rest.astype(jnp.bfloat16)
                low = (rest - mid.astype(jnp.float32)).astype(jnp.bfloat16)
                got.append((choose(high) + choose(mid)) + choose(low))
            which = choose(kinds[...].astype(jnp.float32).astype(jnp.bfloat16))
            for u in range(halo_tiles):
                part = slice(u * TILE, (u + 1) * TILE)
                spot = tiles + side * halo_tiles + u
                kind = jnp.broadcast_to(which[:, part].astype(jnp.int32), (8, TILE))
                values = [g[:, part] for g in got]
                values += [lookup(wells, kind)[0:1], lookup(radii, kind)[0:1]]
                inside = jnp.full((1, TILE), edge_ref[side]) > 0
                for f in range(5):
                    feat_ref[m, spot, f:f + 1, :] = jnp.where(inside, values[f], 0.0)

    ext = tiles + 2 * halo_tiles
    for m in range(images):
        def spread(n, carry):
            turned = feat_ref[m, n].T
            for f in range(5):
                cols_ref[f, n] = jnp.broadcast_to(turned[:, f:f + 1], (TILE, TILE))
            return carry

        lax.fori_loop(0, ext, spread, 0)

        def tile_step(t, energy):
            own = [jnp.broadcast_to(feat_ref[m, t, f:f + 1, :], (8, TILE)) for f in range(5)]
            zero = jnp.zeros((8, TILE), jnp.float32)
            fx, fy, fz, en = zero, zero, zero, zero
            for k in range(PARTNERS):
                p = lists_ref[m, k, t]
                for j in range(TILE // 8):
                    part = [cols_ref[f, p, j * 8:(j + 1) * 8, :] for f in range(5)]
                    dx, dy, dz = own[0] - part[0], own[1] - part[1], own[2] - part[2]
                    reach = own[4] + part[4]
                    reach_sq = reach * reach
                    den = (dx * dx + dy * dy) + (dz * dz + reach_sq)
                    inv = pltpu.reciprocal(den, approx=True)
                    ratio = reach_sq * inv
                    cubed = ratio * ratio * ratio
                    a = part[3] * cubed
                    b = a * cubed
                    e = b - a
                    en = en + e
                    c = (b + e) * inv
                    fx = fx + c * dx
                    fy = fy + c * dy
                    fz = fz + c * dz
            scale = 24.0 * feat_ref[m, t, 3:4, :]
            force_ref[m, :, pl.ds(pl.multiple_of(t * TILE, TILE), TILE)] = jnp.concatenate(
                [jnp.sum(f, axis=0, keepdims=True) * scale for f in (fx, fy, fz)], axis=0
            )
            return energy + 4.0 * own[3] * en

        energy_ref[m] = lax.fori_loop(0, tiles, tile_step, jnp.zeros((8, TILE), jnp.float32))


def exchange_kernel(
    n_space, n_image, coords_ref, types_ref, low_ref, low_types_ref, up_ref, up_types_ref,
    before_ref, after_ref, send_sem, recv_sem,
):
    slab, image = lax.axis_index("space"), lax.axis_index("image")
    last = coords_ref.shape[0] - 1
    links = (
        (slab < n_space - 1, slab > 0, "space", slab, 1,
         ((coords_ref, low_ref), (types_ref, low_types_ref))),
        (slab > 0, slab < n_space - 1, "space", slab, -1,
         ((coords_ref, up_ref), (types_ref, up_types_ref))),
        (image < n_image - 1, image > 0, "image", image, 1,
         ((coords_ref.at[pl.ds(last, 1)], before_ref),)),
        (image > 0, image < n_image - 1, "image", image, -1,
         ((coords_ref.at[pl.ds(0, 1)], after_ref),)),
    )
    barrier = pltpu.get_barrier_semaphore()
    for sends, _, axis, here, step, _ in links:
        @pl.when(sends)
        def _(axis=axis, here=here, step=step):
            pl.semaphore_signal(
                barrier, inc=1, device_id={axis: here + step}, device_id_type=pl.DeviceIdType.MESH
            )
    peers = sum(link[0].astype(jnp.int32) for link in links)
    pl.semaphore_wait(barrier, peers)

    slot = 0
    waits = []
    for sends, gets, axis, here, step, pairs in links:
        copies = []
        for src, dst in pairs:
            copies.append(pltpu.make_async_remote_copy(
                src_ref=src, dst_ref=dst, send_sem=send_sem.at[slot], recv_sem=recv_sem.at[slot],
                device_id={axis: here + step}, device_id_type=pl.DeviceIdType.MESH,
            ))
            slot += 1
        @pl.when(sends)
        def _(copies=copies):
            for c in copies:
                c.start()
        @pl.when(jnp.logical_not(gets))
        def _(pairs=pairs):
            for _, dst in pairs:
                dst[...] = jnp.zeros_like(dst)
        waits.append((sends, gets, copies))
    for sends, gets, copies in waits:
        @pl.when(gets)
        def _(copies=copies):
            for c in copies:
                c.wait_recv()
    for sends, gets, copies in waits:
        @pl.when(sends)
        def _(copies=copies):
            for c in copies:
                c.wait_send()


def exchange(coords, types, n_space, n_image):
    vmem = pl.BlockSpec(memory_space=pltpu.VMEM)
    whole = jax.ShapeDtypeStruct(coords.shape, coords.dtype)
    kinds = jax.ShapeDtypeStruct(types.shape, types.dtype)
    rim = jax.ShapeDtypeStruct((1,) + coords.shape[1:], coords.dtype)
    return pl.pallas_call(
        functools.partial(exchange_kernel, n_space, n_image),
        out_shape=(whole, kinds, whole, kinds, rim, rim),
        in_specs=[vmem, vmem],
        out_specs=(vmem,) * 6,
        scratch_shapes=[pltpu.SemaphoreType.DMA((6,)), pltpu.SemaphoreType.DMA((6,))],
        compiler_params=pltpu.CompilerParams(collective_id=0, has_side_effects=True),
    )(coords, types)


def pair_forces(lists, edge, coords, types, low, low_types, up, up_types, halo, table):
    images, _, tiles, _ = coords.shape
    atoms = tiles * TILE
    ext = tiles + 2 * (halo.shape[2] // TILE)
    vmem = pl.BlockSpec(memory_space=pltpu.VMEM)
    smem = pl.BlockSpec(memory_space=pltpu.SMEM)
    return pl.pallas_call(
        pair_kernel,
        out_shape=(
            jax.ShapeDtypeStruct((images, 3, atoms), jnp.float32),
            jax.ShapeDtypeStruct((images, 8, TILE), jnp.float32),
        ),
        in_specs=[smem, smem] + [vmem] * 8,
        out_specs=(vmem, vmem),
        scratch_shapes=[
            pltpu.VMEM((2, tiles, TILE), jnp.float32),
            pltpu.VMEM((images, ext, 8, TILE), jnp.float32),
            pltpu.VMEM((5, ext, TILE, TILE), jnp.float32),
        ],
        compiler_params=pltpu.CompilerParams(vmem_limit_bytes=40 * 1024 * 1024),
    )(lists, edge, coords, types, low, low_types, up, up_types, halo, table)


def image_total(values):
    return jnp.sum(values, axis=(1, 2))


def body(
    coords, ref_coords, restraint, atom_types, well_table, radius_table, tile_lists, halo_index
):
    img_local, _, atoms_local = coords.shape
    tiles_local = atoms_local // TILE
    n_space = lax.axis_size("space")
    n_image = lax.axis_size("image")
    types = atom_types.reshape(tiles_local, TILE)
    table = jnp.pad(
        jnp.stack([well_table, radius_table]), ((0, 0), (0, TILE - well_table.shape[0]))
    )
    tiled = coords.reshape(img_local, 3, tiles_local, TILE)
    low, low_types, high, high_types, before, after = exchange(tiled, types, n_space, n_image)
    before = before.reshape(1, 3, atoms_local)
    after = after.reshape(1, 3, atoms_local)
    slab = lax.axis_index("space")
    edge = jnp.stack([slab > 0, slab < n_space - 1]).astype(jnp.int32)
    halo = halo_index
    pair_force, pair_energy = pair_forces(
        tile_lists, edge, tiled, types, low, low_types, high, high_types, halo, table
    )
    offset = coords - ref_coords[None]
    forces = pair_force - restraint[None, None] * offset
    local_energy = 0.5 * image_total(pair_energy) + 0.5 * image_total(
        restraint[None, None] * offset * offset
    )
    rims = jnp.concatenate([before, coords, after], axis=0)
    ahead = rims[2:] - coords
    behind = coords - rims[:-2]
    ahead_sq, behind_sq, cross, force_ahead, force_behind, energy_sum = lax.psum(
        (
            image_total(ahead * ahead),
            image_total(behind * behind),
            image_total(ahead * behind),
            image_total(forces * ahead),
            image_total(forces * behind),
            local_energy,
        ),
        "space",
    )
    ahead_norm = jnp.sqrt(ahead_sq + small_eps)
    behind_norm = jnp.sqrt(behind_sq + small_eps)
    tan_sq = (
        ahead_sq / (ahead_norm * ahead_norm)
        + 2.0 * cross / (ahead_norm * behind_norm)
        + behind_sq / (behind_norm * behind_norm)
    )
    tan_norm = jnp.sqrt(tan_sq + small_eps)
    ahead_len = ahead_norm[:, None, None]
    behind_len = behind_norm[:, None, None]
    tan_len = tan_norm[:, None, None]
    unit = (ahead / ahead_len + behind / behind_len) / tan_len
    along = ((force_ahead / ahead_norm + force_behind / behind_norm) / tan_norm)[:, None, None]
    banded = forces - along * unit + spring_k * (ahead_len - behind_len) * unit
    total_images = img_local * n_image
    order = lax.axis_index("image") * img_local + jnp.arange(img_local, dtype=jnp.int32)
    ends = ((order == 0) | (order == total_images - 1))[:, None, None]
    neb_force = jnp.where(ends, forces, banded)
    energies = energy_sum / (atoms_local * n_space)
    return (neb_force, energies)


def solution(mesh):
    in_specs = (
        P("image", None, "space"),
        P(None, "space"),
        P("space"),
        P("space"),
        P(),
        P(),
        P("image", None, "space"),
        P("image", None, "space"),
    )
    out_specs = (P("image", None, "space"), P("image"))
    return jax.shard_map(body, mesh=mesh, in_specs=in_specs, out_specs=out_specs, check_vma=False)
```
